32 devices in a mesh: ctx: 8 (over z, x), dp: 4 (over y, core).
Axes of the slice: x: 2, y: 2, z: 4, core: 2. Of those that a mesh axis runs over, the one named last changes fastest.
Arguments:
- tokens: bfloat16 [4, 4096, 512], P('dp', 'ctx'), may hold values from -6 to 6
- segment_ids: int32 [4, 4096], P('dp', 'ctx'), may hold values from 0 to 3, never falling along the last dimension, each value on 1 to 2048 neighbouring positions
- w_query: bfloat16 [512, 512], replicated, may hold values from -0.25 to 0.25
- w_key: bfloat16 [512, 512], replicated, may hold values from -0.25 to 0.25
- w_value: bfloat16 [512, 512], replicated, may hold values from -0.25 to 0.25
- w_out: bfloat16 [512, 512], replicated, may hold values from -0.25 to 0.25
- grad_out: bfloat16 [4, 4096, 512], P('dp', 'ctx'), may hold values from -6 to 6
Outputs:
- input_grad: bfloat16 [4, 4096, 512], P('dp', 'ctx')
- grad_w_query: bfloat16 [512, 512], replicated
- grad_w_key: bfloat16 [512, 512], replicated
- grad_w_value: bfloat16 [512, 512], replicated
- grad_w_out: bfloat16 [512, 512], replicated
The draws below stay inside these ranges and needn't reach their ends.
Inputs may be any that keep to these rules, and one draw needn't show every extreme that they name: `segment_ids`: each drive log is a run of consecutive tokens of at most 2048 tokens.
All inputs are finite; a program needn't handle non-finite values.
Results may differ from the reference program's by a relative error of at most 0.006.
The reference program's roundings to bfloat16 on the way (of `dattn`, `probb`, `attended`, `dscore` and `dquery`) count: a program that leaves them out, or rounds other values in their place, can miss the bound.
Values may be sent and summed in bfloat16 or wider, within the bound.
A program may use at most 64 MiB of HBM per device.

```python
import math
import jax
import jax.numpy as jnp
import numpy as np
from jax import lax

D = 512
H = 8
HD = 64
WINDOW = 128
TOK_DEV = 512
CONTEXT = 4096
BATCH = 4
N_CTX = 8


def draw_tokens(key, part):
    key = jax.random.fold_in(key, 7)
    first = jax.random.fold_in(key, 0)
    values = jax.random.normal(first, (BATCH, CONTEXT, D), jnp.float32)
    return jnp.clip(values, -6.0, 6.0).astype(jnp.bfloat16)


def block_scale(key, dims, shards, low, top_value):
    def one(position, blocks):
        steps = jax.random.uniform(jax.random.fold_in(jax.random.fold_in(key, 6), position), (blocks,), jnp.float32, low / len(shards), top_value / len(shards))
        return jnp.repeat(jnp.exp(steps), dims[position] // blocks).reshape((-1,) + (1,) * (len(dims) - position - 1))

    gain = one(*shards[0])
    for cut in shards[1:]:
        gain = gain * one(*cut)
    return gain


def length_profile(count, total, reach, slope):
    loads = [(1 << 20) // math.isqrt(grade ** slope) + 1 for grade in range(2, count + 1)]
    spare, given = total - reach - (count - 1), [1] * (count - 1)
    while spare > 0:
        movable = [i for i in range(count - 1) if given[i] < reach]
        pool, budget = sum([loads[i] for i in movable]), spare
        for i in movable:
            extra = min(reach - given[i], max(1, budget * loads[i] // pool), spare)
            given[i] = given[i] + extra
            spare = spare - extra
    return np.array([reach] + given)


def uneven_parts(stream_key, count, total, bound, lean):
    if count == 2:
        one = jax.random.randint(stream_key, (), max(1, total - bound), min(bound, total - 1) + 1)
        return jnp.stack([one, total - one])
    lengths = jnp.asarray(length_profile(count, total, bound, lean), jnp.int32)
    pairs = (count - 1) // 2
    donor, taker = lengths[1:1 + 2 * pairs:2], lengths[2:2 + 2 * pairs:2]
    margin = jnp.minimum(donor - 1, bound - taker)
    shifted = jax.random.randint(jax.random.fold_in(stream_key, 1), (pairs,), 0, 1 << 20) % (margin + 1)
    lengths = lengths.at[1:1 + 2 * pairs:2].set(donor - shifted).at[2:2 + 2 * pairs:2].set(taker + shifted)
    return lengths[jax.random.permutation(jax.random.fold_in(stream_key, 2), count)]


def scatter_about(rng, dims, width, reach, cuts=(), kind=jnp.bfloat16):
    factor_of = block_scale(rng, dims, cuts, -0.22, 0.18) if cuts else 1.0
    values = jax.random.normal(rng, dims, jnp.float32) * width * factor_of
    return jnp.minimum(jnp.maximum(values, -reach), reach).astype(kind)


def setup_inputs(seed: int = 0) -> dict:
    seeds = jax.random.split(jax.random.key(seed), 8)
    return {
        "tokens": draw_tokens(jax.random.fold_in(seeds[7], 71), 0),
        "segment_ids": jax.vmap(lambda own: jnp.searchsorted(jnp.cumsum(uneven_parts(own, N_CTX // 2, CONTEXT, 4 * TOK_DEV, 2)), jnp.arange(CONTEXT), side="right"))(jax.random.split(seeds[1], BATCH)).reshape((BATCH, CONTEXT)).astype(jnp.int32),
        "w_query": scatter_about(seeds[2], (D, D), D ** -0.5, 0.25),
        "w_key": scatter_about(seeds[3], (D, D), D ** -0.5, 0.25),
        "w_value": scatter_about(seeds[4], (D, D), D ** -0.5, 0.25),
        "w_out": scatter_about(seeds[5], (D, D), D ** -0.5, 0.25),
        "grad_out": scatter_about(seeds[6], (BATCH, CONTEXT, D), 1.0, 6.0, ((0, 4), (1, 8))),
    }


def mult(form, left, right):
    return jnp.einsum(form, left.astype(jnp.float32), right.astype(jnp.float32))


def attend(query, dattn, keyed, valued, mask):
    scale = float(query.shape[-1]) ** -0.5
    score = mult("qhd,khd->hqk", query, keyed) * scale
    score = jnp.where(mask[None], score, -1e30)
    top = jnp.max(score, axis=-1, keepdims=True)
    weight = jnp.where(mask[None], jnp.exp(score - top), 0.0)
    prob = weight / jnp.sum(weight, axis=-1, keepdims=True)
    probb = prob.astype(jnp.bfloat16)
    attended = mult("hqk,khd->qhd", probb, valued).astype(jnp.bfloat16)
    dprob = mult("qhd,khd->hqk", dattn, valued)
    delta = jnp.sum(dattn.astype(jnp.float32) * attended.astype(jnp.float32), axis=-1)
    dscore = (prob * (dprob - delta.T[:, :, None])).astype(jnp.bfloat16)
    dquery = (mult("hqk,khd->qhd", dscore, keyed) * scale).astype(jnp.bfloat16)
    dkey = (mult("hqk,qhd->khd", dscore, query) * scale).astype(jnp.bfloat16)
    dvalue = mult("hqk,qhd->khd", probb, dattn).astype(jnp.bfloat16)
    return attended, dquery, dkey, dvalue


def reference(tokens, segment_ids, w_query, w_key, w_value, w_out, grad_out):
    blocks = N_CTX
    span = TOK_DEV
    window = WINDOW
    keys_len = span + 2 * window
    flat = tokens.reshape(-1, D)
    dflat = grad_out.reshape(-1, D)

    def project(weight):
        return jnp.dot(flat, weight, preferred_element_type=jnp.float32).astype(jnp.bfloat16).reshape(BATCH, blocks, span, H, HD)

    query = project(w_query)
    keyed = project(w_key)
    valued = project(w_value)
    dattn = jnp.dot(dflat, w_out.T, preferred_element_type=jnp.float32).astype(jnp.bfloat16).reshape(BATCH, blocks, span, H, HD)
    seg = segment_ids.reshape(BATCH, blocks, span)
    query_pos = jnp.arange(span, dtype=jnp.int32)
    key_pos = jnp.arange(keys_len, dtype=jnp.int32) - window
    near = jnp.abs(query_pos[:, None] - key_pos[None, :]) <= window

    def one(index):
        batch = index // blocks
        block = index % blocks
        lower = jnp.maximum(block - 1, 0)
        upper = jnp.minimum(block + 1, blocks - 1)
        keys_all = jnp.concatenate([keyed[batch, lower][span - window:], keyed[batch, block], keyed[batch, upper][:window]], 0)
        values_all = jnp.concatenate([valued[batch, lower][span - window:], valued[batch, block], valued[batch, upper][:window]], 0)
        seg_all = jnp.concatenate([seg[batch, lower][span - window:], seg[batch, block], seg[batch, upper][:window]], 0)
        valid = jnp.concatenate([jnp.full((window,), block > 0), jnp.ones((span,), bool), jnp.full((window,), block < blocks - 1)])
        mask = (seg[batch, block][:, None] == seg_all[None, :]) & valid[None, :] & near
        attended, dquery, dkey, dvalue = attend(query[batch, block], dattn[batch, block], keys_all, values_all, mask)
        return attended.reshape(span, D), dquery.reshape(span, D), dkey.reshape(keys_len, D), dvalue.reshape(keys_len, D)

    attended, dquery, dkey, dvalue = lax.map(one, jnp.arange(BATCH * blocks, dtype=jnp.int32))
    dkey = dkey.reshape(BATCH, blocks, keys_len, D)
    dvalue = dvalue.reshape(BATCH, blocks, keys_len, D)

    def parts(grad):
        own = grad[:, :, window:window + span]
        low_part = jnp.pad(grad[:, :, :window], ((0, 0), (0, 0), (span - window, 0), (0, 0)))
        high_part = jnp.pad(grad[:, :, window + span:], ((0, 0), (0, 0), (0, span - window), (0, 0)))
        from_upper = jnp.roll(low_part, -1, axis=1)
        from_lower = jnp.roll(high_part, 1, axis=1)
        return [p.reshape(-1, D) for p in (own, from_upper, from_lower)]

    key_parts = parts(dkey)
    value_parts = parts(dvalue)
    dquery = dquery.reshape(-1, D)
    attended = attended.reshape(-1, D)
    total = jnp.dot(dquery, w_query.T, preferred_element_type=jnp.float32)
    grad_wk = jnp.zeros((D, D), jnp.float32)
    grad_wv = jnp.zeros((D, D), jnp.float32)
    for piece_k, piece_v in zip(key_parts, value_parts):
        total = total + jnp.dot(piece_k, w_key.T, preferred_element_type=jnp.float32)
        total = total + jnp.dot(piece_v, w_value.T, preferred_element_type=jnp.float32)
        grad_wk = grad_wk + jnp.dot(flat.T, piece_k, preferred_element_type=jnp.float32)
        grad_wv = grad_wv + jnp.dot(flat.T, piece_v, preferred_element_type=jnp.float32)
    grad_wq = jnp.dot(flat.T, dquery, preferred_element_type=jnp.float32)
    grad_wo = jnp.dot(attended.T, dflat, preferred_element_type=jnp.float32)
    input_grad = total.astype(jnp.bfloat16).reshape(BATCH, CONTEXT, D)
    return (input_grad, grad_wq.astype(jnp.bfloat16), grad_wk.astype(jnp.bfloat16), grad_wv.astype(jnp.bfloat16), grad_wo.astype(jnp.bfloat16))
```

```python
import functools

import jax
import jax.numpy as jnp
from jax import lax
from jax.experimental import pallas as pl
from jax.experimental.pallas import tpu as pltpu
from jax.sharding import PartitionSpec as P

HD = 64
WINDOW = 128
PAIR = 128
TILE_ROWS = 16
MESH = pl.DeviceIdType.MESH
F32 = jnp.float32
BF16 = jnp.bfloat16


def nn(left, right):
    return lax.dot_general(left, right, (((1,), (0,)), ((), ())), preferred_element_type=F32)


def nt(left, right):
    return lax.dot_general(left, right, (((1,), (1,)), ((), ())), preferred_element_type=F32)


def tn(left, right):
    return lax.dot_general(left, right, (((0,), (0,)), ((), ())), preferred_element_type=F32)


def wrap(index, count):
    return lax.rem(index + count, count)


def kernel(
    n_ctx, n_dp, reduced,
    tok, seg_row, w_q, w_k, w_v, w_o, dout,
    out, grads,
    halo, seg_halo, seg_own, tok_t, query, dattn, keyed, valued, bias,
    dq, dk, dv, acc_k, acc_v, att,
    side_send, side_recv,
    total, send, recv_a, recv_b, recv_c, recv_d,
    halo_s, halo_r, seg_s, seg_r, side_s, side_r, rs_s, rs_r, ag_s, ag_r,
):
    span, width = tok.shape
    win = WINDOW
    blocks = span // win
    pairs = width // PAIR
    ctx = lax.axis_index("ctx")
    dp = lax.axis_index("dp")
    up = (wrap(ctx + 1, n_ctx), dp)
    down = (wrap(ctx - 1, n_ctx), dp)

    core = lax.rem(dp, 2)
    y = lax.div(dp, 2)
    x = lax.rem(ctx, 2)
    z = lax.div(ctx, 2)
    nz = n_ctx // 2
    to_core = (ctx, dp + 1 - 2 * core)
    to_y = (ctx, lax.rem(dp + 2, 4))
    to_x = (ctx + 1 - 2 * x, dp)

    def to_z(step):
        return (lax.rem(ctx + 2 * step, n_ctx), dp)

    partners = [up, down]
    if reduced:
        partners += [to_core, to_y] + [to_z(step) for step in range(1, nz)]
    barrier = pltpu.get_barrier_semaphore()
    for partner in partners:
        pl.semaphore_signal(barrier, inc=1, device_id=partner, device_id_type=MESH)

    seg_own[...] = jnp.broadcast_to(seg_row[...], seg_own.shape)
    pl.semaphore_wait(barrier, len(partners))

    def remote(src, dst, s, r, device):
        copy = pltpu.make_async_remote_copy(
            src_ref=src, dst_ref=dst, send_sem=s, recv_sem=r, device_id=device, device_id_type=MESH
        )
        copy.start()
        return copy

    first = [
        remote(tok.at[pl.ds(span - win, win)], halo.at[0], halo_s.at[0], halo_r.at[0], up),
        remote(tok.at[pl.ds(0, win)], halo.at[1], halo_s.at[1], halo_r.at[1], down),
        remote(seg_own, seg_halo.at[0], seg_s.at[0], seg_r.at[0], up),
        remote(seg_own, seg_halo.at[1], seg_s.at[1], seg_r.at[1], down),
    ]

    query[...] = nn(tok[...], w_q[...]).astype(BF16)
    keyed[pl.ds(win, span)] = nn(tok[...], w_k[...]).astype(BF16)
    valued[pl.ds(win, span)] = nn(tok[...], w_v[...]).astype(BF16)
    dattn[...] = nt(dout[...], w_o[...]).astype(BF16)
    tok_t[:, pl.ds(win, span)] = tok[...].T

    for copy in first:
        copy.wait()
    for side, start in ((0, 0), (1, win + span)):
        rows = halo[side]
        keyed[pl.ds(start, win)] = nn(rows, w_k[...]).astype(BF16)
        valued[pl.ds(start, win)] = nn(rows, w_v[...]).astype(BF16)
        tok_t[:, pl.ds(start, win)] = rows.T

    own = seg_row[...].astype(F32)
    low = jnp.where(ctx > 0, seg_halo[0, 0:1, span - win :].astype(F32), -1.0)
    high = jnp.where(ctx < n_ctx - 1, seg_halo[1, 0:1, :win].astype(F32), -1.0)
    seg_all = jnp.concatenate([low, own, high], axis=1)
    q_pos = lax.broadcasted_iota(jnp.int32, (win, 3 * win), 0)
    k_pos = lax.broadcasted_iota(jnp.int32, (win, 3 * win), 1)
    near = (k_pos >= q_pos) & (k_pos <= q_pos + 2 * win)
    for i in range(blocks):
        column = jnp.broadcast_to(own[:, i * win : (i + 1) * win], (win, win)).T
        column = jnp.concatenate([column] * 3, axis=1)
        same = column == seg_all[:, i * win : (i + 3) * win]
        bias[i] = jnp.where(near & same, 0.0, -1e30)

    scale = float(HD) ** (-0.5)
    lane = lax.broadcasted_iota(jnp.int32, (win, PAIR), 1)
    left = lane < HD

    def stack(rows):
        zero = jnp.zeros_like(rows)
        return jnp.concatenate([jnp.where(left, rows, zero), jnp.where(left, zero, rows)], axis=0)

    def join(rows):
        return jnp.where(left, rows[:win], rows[win:])

    def attend(p, i):
        cols = pl.ds(p * PAIR, PAIR)
        here = pl.ds(i * win, win)
        around = pl.ds(i * win, 3 * win)
        q2 = stack(query[here, cols])
        d2 = stack(dattn[here, cols])
        k2 = keyed[around, cols]
        v2 = valued[around, cols]
        mask = bias[i]
        score = nt(q2, k2) * scale + jnp.concatenate([mask, mask], axis=0)
        top = jnp.max(score, axis=-1, keepdims=True)
        weight = jnp.exp(score - top)
        prob = weight * (1.0 / jnp.sum(weight, axis=-1, keepdims=True))
        probb = prob.astype(BF16)
        attended = nn(probb, v2).astype(BF16)
        att[here, :] = join(attended)
        delta = jnp.sum(d2.astype(F32) * attended.astype(F32), axis=-1, keepdims=True)
        dscore = (prob * (nt(d2, v2) - delta)).astype(BF16)
        dq[here, cols] = (join(nn(dscore, k2)) * scale).astype(BF16)
        part_k = tn(dscore, q2)
        part_v = tn(probb, d2)
        if i == 0:
            acc_k[around] = part_k
            acc_v[around] = part_v
        else:
            kept = pl.ds(i * win, 2 * win)
            fresh = pl.ds((i + 2) * win, win)
            acc_k[kept] += part_k[: 2 * win]
            acc_v[kept] += part_v[: 2 * win]
            acc_k[fresh] = part_k[2 * win :]
            acc_v[fresh] = part_v[2 * win :]

    sides = []

    def finish(p):
        cols = pl.ds(p * PAIR, PAIR)
        dk[:, cols] = (acc_k[...] * scale).astype(BF16)
        dv[:, cols] = acc_v[...].astype(BF16)
        for side, start, device in ((0, 0, down), (1, win + span, up)):
            side_send[p, side, 0] = dk[pl.ds(start, win), cols]
            side_send[p, side, 1] = dv[pl.ds(start, win), cols]
            sides.append(
                remote(
                    side_send.at[p, side], side_recv.at[p, side],
                    side_s.at[p, side], side_r.at[p, side], device,
                )
            )
        values = (
            nn(tok_t[:, pl.ds(win, span)], dq[:, cols]),
            nn(tok_t[...], dk[:, cols]),
            nn(tok_t[...], dv[:, cols]),
            tn(dout[...], att[...]),
        )
        for m, value in enumerate(values):
            if reduced:
                total[p, m] = value
            else:
                grads[p, m] = value

    rows_a, rows_b, rows_c = width // 2, width // 4, width // 8
    rows_d = width // (8 * nz)
    plans = []
    for p in range(pairs):
        (bit_b, dev_b), (bit_c, dev_c) = ((x, to_x), (y, to_y)) if p % 2 == 0 else ((y, to_y), (x, to_x))
        base_a = core * rows_a
        base_b = base_a + bit_b * rows_b
        base_c = base_b + bit_c * rows_c
        base_d = base_c + z * rows_d
        plans.append((
            (rows_a, base_a, (1 - core) * rows_a, to_core, recv_a),
            (rows_b, base_b, base_a + (1 - bit_b) * rows_b, dev_b, recv_b),
            (rows_c, base_c, base_b + (1 - bit_c) * rows_c, dev_c, recv_c),
            base_d,
        ))

    flying = {}

    def window(start, rows):
        return pl.ds(pl.multiple_of(start, TILE_ROWS), rows)

    def push(p, level):
        rows, _, other, device, landing = plans[p][level]
        part = window(other, rows)
        send[p, :, part, :] = total[p, :, part, :].astype(BF16)
        flying[p, level] = remote(
            send.at[p, :, part, :], landing.at[p], rs_s.at[p, level], rs_r.at[p, level], device
        )

    def take(p, level):
        rows, base, _, _, landing = plans[p][level]
        flying[p, level].wait()
        part = window(base, rows)
        total[p, :, part, :] += landing[p].astype(F32)

    def push_z(p):
        base_c = plans[p][2][1]
        part = window(base_c, rows_c)
        send[p, :, part, :] = total[p, :, part, :].astype(BF16)
        for step in range(1, nz):
            there = base_c + lax.rem(z + step, nz) * rows_d
            flying[p, 2 + step] = remote(
                send.at[p, :, window(there, rows_d), :], recv_d.at[p, step - 1],
                rs_s.at[p, 2 + step], rs_r.at[p, 2 + step], to_z(step),
            )

    def take_z(p):
        part = window(plans[p][3], rows_d)
        value = total[p, :, part, :]
        for step in range(1, nz):
            flying[p, 2 + step].wait()
            value = value + recv_d[p, step - 1].astype(F32)
        grads[p, :, part, :] = value.astype(BF16)
        for step in range(1, nz):
            flying[p, "z", step] = remote(
                grads.at[p, :, part, :], grads.at[p, :, part, :],
                ag_s.at[p, 2 + step], ag_r.at[p, 2 + step], to_z(step),
            )

    def spread(p, level):
        rows, base, _, device, _ = plans[p][level]
        part = window(base, rows)
        flying[p, "g", level] = remote(
            grads.at[p, :, part, :], grads.at[p, :, part, :],
            ag_s.at[p, level], ag_r.at[p, level], device,
        )

    def event(p, number):
        if number == 0:
            push(p, 0)
        elif number in (1, 2):
            take(p, number - 1)
            push(p, number)
        elif number == 3:
            take(p, 2)
            push_z(p)
        elif number == 4:
            take_z(p)
        elif number == 5:
            for step in range(1, nz):
                flying[p, "z", step].wait()
            spread(p, 2)
        elif number in (6, 7):
            flying[p, "g", 8 - number].wait()
            spread(p, 7 - number)
        elif number == 8:
            flying[p, "g", 0].wait()

    def tick(slot):
        if reduced:
            for p in range(pairs):
                number = slot - blocks * (p + 1)
                if 0 <= number <= 8:
                    event(p, number)

    slot = 0
    for p in range(pairs):
        for i in range(blocks):
            tick(slot)
            attend(p, i)
            slot += 1
        finish(p)
    for i in range(blocks):
        tick(slot)
        here = pl.ds(i * win, win)
        there = pl.ds((i + 1) * win, win)
        value = nt(dq[here], w_q[...]) + nt(dk[there], w_k[...]) + nt(dv[there], w_v[...])
        if i == 0:
            for copy in sides:
                copy.wait()
        if i in (0, blocks - 1):
            for side in ((1,) if i == 0 else (0,)):
                part_k = jnp.concatenate([side_recv[p, side, 0] for p in range(pairs)], axis=1)
                part_v = jnp.concatenate([side_recv[p, side, 1] for p in range(pairs)], axis=1)
                value = value + nt(part_k, w_k[...]) + nt(part_v, w_v[...])
        out[here] = value.astype(BF16)
        slot += 1
    while slot <= blocks * pairs + 8:
        tick(slot)
        slot += 1


def on_device(tokens, segment_ids, w_query, w_key, w_value, w_out, grad_out):
    span, width = tokens.shape[1:]
    n_ctx, n_dp = lax.axis_size("ctx"), lax.axis_size("dp")
    pairs = width // PAIR
    nz = n_ctx // 2
    reduced = n_dp == 4 and n_ctx % 2 == 0 and width // (8 * nz) >= TILE_ROWS
    ext = span + 2 * WINDOW
    vmem = pltpu.VMEM
    dma = pltpu.SemaphoreType.DMA
    few = nz if reduced else 2

    def red(*shape):
        return vmem(shape if reduced else (TILE_ROWS, 128), BF16)

    scratch = [
        vmem((2, WINDOW, width), BF16),
        vmem((2, 8, span), jnp.int32),
        vmem((8, span), jnp.int32),
        vmem((width, ext), BF16),
        vmem((span, width), BF16),
        vmem((span, width), BF16),
        vmem((ext, width), BF16),
        vmem((ext, width), BF16),
        vmem((span // WINDOW, WINDOW, 3 * WINDOW), F32),
        vmem((span, width), BF16),
        vmem((ext, width), BF16),
        vmem((ext, width), BF16),
        vmem((ext, PAIR), F32),
        vmem((ext, PAIR), F32),
        vmem((span, PAIR), BF16),
        vmem((pairs, 2, 2, WINDOW, PAIR), BF16),
        vmem((pairs, 2, 2, WINDOW, PAIR), BF16),
        vmem((pairs, 4, width, PAIR) if reduced else (8, 128), F32),
        red(pairs, 4, width, PAIR),
        red(pairs, 4, width // 2, PAIR),
        red(pairs, 4, width // 4, PAIR),
        red(pairs, 4, width // 8, PAIR),
        red(pairs, few - 1, 4, width // (8 * few), PAIR),
        dma((2,)), dma((2,)), dma((2,)), dma((2,)),
        dma((pairs, 2)), dma((pairs, 2)),
        dma((pairs, 2 + few)), dma((pairs, 2 + few)),
        dma((pairs, 2 + few)), dma((pairs, 2 + few)),
    ]
    total, grads = pl.pallas_call(
        functools.partial(kernel, n_ctx, n_dp, reduced),
        out_shape=(
            jax.ShapeDtypeStruct((span, width), BF16),
            jax.ShapeDtypeStruct((pairs, 4, width, PAIR), BF16 if reduced else F32),
        ),
        in_specs=[pl.BlockSpec(memory_space=pltpu.VMEM)] * 7,
        out_specs=(pl.BlockSpec(memory_space=pltpu.VMEM),) * 2,
        scratch_shapes=scratch,
        compiler_params=pltpu.CompilerParams(
            collective_id=0, has_side_effects=True, vmem_limit_bytes=48 * 1024 * 1024
        ),
    )(tokens[0], segment_ids, w_query, w_key, w_value, w_out, grad_out[0])
    if not reduced:
        grads = lax.psum(grads, ("ctx", "dp")).astype(BF16)
    merged = jnp.transpose(grads[:, :3], (1, 2, 0, 3)).reshape(3, width, width)
    grad_o = jnp.transpose(grads[:, 3], (0, 2, 1)).reshape(width, width)
    return (total[None], merged[0], merged[1], merged[2], grad_o)


def solution(mesh):
    return jax.shard_map(
        on_device,
        mesh=mesh,
        in_specs=(P("dp", "ctx", None), P("dp", "ctx"), P(), P(), P(), P(), P("dp", "ctx", None)),
        out_specs=(P("dp", "ctx", None), P(), P(), P(), P()),
        check_vma=False,
    )
```

```python
import functools

import jax
import jax.numpy as jnp
from jax import lax
from jax.experimental import pallas as pl
from jax.experimental.pallas import tpu as pltpu
from jax.sharding import PartitionSpec as P

HD = 64
WINDOW = 128
PAIR = 128
TILE_ROWS = 16
MESH = pl.DeviceIdType.MESH
F32 = jnp.float32
BF16 = jnp.bfloat16


def nn(left, right):
    return lax.dot_general(left, right, (((1,), (0,)), ((), ())), preferred_element_type=F32)


def nt(left, right):
    return lax.dot_general(left, right, (((1,), (1,)), ((), ())), preferred_element_type=F32)


def tn(left, right):
    return lax.dot_general(left, right, (((0,), (0,)), ((), ())), preferred_element_type=F32)


def wrap(index, count):
    return lax.rem(index + count, count)


def kernel(
    n_ctx, n_dp, reduced,
    tok_hbm, seg_hbm, wq_hbm, wk_hbm, wv_hbm, wo_hbm, dout_hbm,
    out, grads,
    tok, seg_row, w_q, w_k, w_v, w_o, dout, load,
    halo, seg_halo, seg_own, tok_t, query, dattn, keyed, valued, bias,
    dq, dk, dv, acc_k, acc_v, att,
    side_send, side_recv,
    total, send, recv_a, recv_b, recv_c, recv_d,
    halo_s, halo_r, seg_s, seg_r, side_s, side_r, rs_s, rs_r, ag_s, ag_r,
):
    span, width = tok.shape
    win = WINDOW
    loads = {}
    for n, (name, src, dst) in enumerate((
        ("seg", seg_hbm, seg_row), ("tok", tok_hbm, tok), ("q", wq_hbm, w_q), ("k", wk_hbm, w_k),
        ("v", wv_hbm, w_v), ("o", wo_hbm, w_o), ("dout", dout_hbm, dout),
    )):
        loads[name] = pltpu.make_async_copy(src, dst, load.at[n])
        loads[name].start()
    blocks = span // win
    pairs = width // PAIR
    ctx = lax.axis_index("ctx")
    dp = lax.axis_index("dp")
    up = (wrap(ctx + 1, n_ctx), dp)
    down = (wrap(ctx - 1, n_ctx), dp)

    core = lax.rem(dp, 2)
    y = lax.div(dp, 2)
    x = lax.rem(ctx, 2)
    z = lax.div(ctx, 2)
    nz = n_ctx // 2
    to_core = (ctx, dp + 1 - 2 * core)
    to_y = (ctx, lax.rem(dp + 2, 4))
    to_x = (ctx + 1 - 2 * x, dp)

    def to_z(step):
        return (lax.rem(ctx + 2 * step, n_ctx), dp)

    partners = [up, down]
    if reduced:
        partners += [to_core, to_y] + [to_z(step) for step in range(1, nz)]
    barrier = pltpu.get_barrier_semaphore()
    for partner in partners:
        pl.semaphore_signal(barrier, inc=1, device_id=partner, device_id_type=MESH)

    loads["seg"].wait()
    seg_own[...] = jnp.broadcast_to(seg_row[...], seg_own.shape)
    pl.semaphore_wait(barrier, len(partners))

    def remote(src, dst, s, r, device):
        copy = pltpu.make_async_remote_copy(
            src_ref=src, dst_ref=dst, send_sem=s, recv_sem=r, device_id=device, device_id_type=MESH
        )
        copy.start()
        return copy

    first = [
        remote(tok_hbm.at[pl.ds(span - win, win)], halo.at[0], halo_s.at[0], halo_r.at[0], up),
        remote(tok_hbm.at[pl.ds(0, win)], halo.at[1], halo_s.at[1], halo_r.at[1], down),
        remote(seg_own, seg_halo.at[0], seg_s.at[0], seg_r.at[0], up),
        remote(seg_own, seg_halo.at[1], seg_s.at[1], seg_r.at[1], down),
    ]

    loads["tok"].wait()
    tok_t[:, pl.ds(win, span)] = tok[...].T
    loads["q"].wait()
    query[...] = nn(tok[...], w_q[...]).astype(BF16)
    loads["k"].wait()
    keyed[pl.ds(win, span)] = nn(tok[...], w_k[...]).astype(BF16)
    loads["v"].wait()
    valued[pl.ds(win, span)] = nn(tok[...], w_v[...]).astype(BF16)
    loads["o"].wait()
    loads["dout"].wait()
    dattn[...] = nt(dout[...], w_o[...]).astype(BF16)

    scale = float(HD) ** (-0.5)
    lane = lax.broadcasted_iota(jnp.int32, (win, PAIR), 1)
    left = lane < HD

    def stack(rows):
        zero = jnp.zeros_like(rows)
        return jnp.concatenate([jnp.where(left, rows, zero), jnp.where(left, zero, rows)], axis=0)

    def join(rows):
        return jnp.where(left, rows[:win], rows[win:])

    def attend(p, i):
        cols = pl.ds(p * PAIR, PAIR)
        here = pl.ds(i * win, win)
        around = pl.ds(i * win, 3 * win)
        q2 = stack(query[here, cols])
        d2 = stack(dattn[here, cols])
        k2 = keyed[around, cols]
        v2 = valued[around, cols]
        mask = bias[i]
        score = nt(q2, k2) * scale + jnp.concatenate([mask, mask], axis=0)
        top = jnp.max(score, axis=-1, keepdims=True)
        weight = jnp.exp(score - top)
        prob = weight * (1.0 / jnp.sum(weight, axis=-1, keepdims=True))
        probb = prob.astype(BF16)
        attended = nn(probb, v2).astype(BF16)
        att[p, here, :] = join(attended)
        delta = jnp.sum(d2.astype(F32) * attended.astype(F32), axis=-1, keepdims=True)
        dscore = (prob * (nt(d2, v2) - delta)).astype(BF16)
        dq[here, cols] = (join(nn(dscore, k2)) * scale).astype(BF16)
        part_k = tn(dscore, q2)
        part_v = tn(probb, d2)
        acc_k[p, around] += part_k
        acc_v[p, around] += part_v

    own = seg_row[...].astype(F32)
    q_pos = lax.broadcasted_iota(jnp.int32, (win, 3 * win), 0)
    k_pos = lax.broadcasted_iota(jnp.int32, (win, 3 * win), 1)
    near = (k_pos >= q_pos) & (k_pos <= q_pos + 2 * win)

    def masked(i, keys):
        column = jnp.broadcast_to(own[:, i * win : (i + 1) * win], (win, win)).T
        column = jnp.concatenate([column] * 3, axis=1)
        bias[i] = jnp.where(near & (column == keys), 0.0, -1e30)

    acc_k[...] = jnp.zeros_like(acc_k)
    acc_v[...] = jnp.zeros_like(acc_v)
    for i in range(1, blocks - 1):
        masked(i, own[:, (i - 1) * win : (i + 2) * win])
        for p in range(pairs):
            attend(p, i)

    for copy in first:
        copy.wait()
    for side, start in ((0, 0), (1, win + span)):
        rows = halo[side]
        keyed[pl.ds(start, win)] = nn(rows, w_k[...]).astype(BF16)
        valued[pl.ds(start, win)] = nn(rows, w_v[...]).astype(BF16)
        tok_t[:, pl.ds(start, win)] = rows.T
    low = jnp.where(ctx > 0, seg_halo[0, 0:1, span - win :].astype(F32), -1.0)
    high = jnp.where(ctx < n_ctx - 1, seg_halo[1, 0:1, :win].astype(F32), -1.0)
    masked(0, jnp.concatenate([low, own[:, : 2 * win]], axis=1))
    masked(blocks - 1, jnp.concatenate([own[:, span - 2 * win :], high], axis=1))

    sides = []

    def finish(p):
        cols = pl.ds(p * PAIR, PAIR)
        dk[:, cols] = (acc_k[p] * scale).astype(BF16)
        dv[:, cols] = acc_v[p].astype(BF16)
        for side, start, device in ((0, 0, down), (1, win + span, up)):
            side_send[p, side, 0] = dk[pl.ds(start, win), cols]
            side_send[p, side, 1] = dv[pl.ds(start, win), cols]
            sides.append(
                remote(
                    side_send.at[p, side], side_recv.at[p, side],
                    side_s.at[p, side], side_r.at[p, side], device,
                )
            )
        values = (
            nn(tok_t[:, pl.ds(win, span)], dq[:, cols]),
            nn(tok_t[...], dk[:, cols]),
            nn(tok_t[...], dv[:, cols]),
        )
        place = total if reduced else grads
        for m, value in enumerate(values):
            place[p, m] = value
        value = tn(att[p], dout[...])
        for j in range(width // PAIR):
            block = pl.ds(j * PAIR, PAIR)
            place[p, 3, block] = value[:, j * PAIR : (j + 1) * PAIR]

    rows_a, rows_b, rows_c = width // 2, width // 4, width // 8
    rows_d = width // (8 * nz)
    plans = []
    for p in range(pairs):
        (bit_b, dev_b), (bit_c, dev_c) = ((y, to_y), (x, to_x))
        base_a = core * rows_a
        base_b = base_a + bit_b * rows_b
        base_c = base_b + bit_c * rows_c
        base_d = base_c + z * rows_d
        plans.append((
            (rows_a, base_a, (1 - core) * rows_a, to_core, recv_a),
            (rows_b, base_b, base_a + (1 - bit_b) * rows_b, dev_b, recv_b),
            (rows_c, base_c, base_b + (1 - bit_c) * rows_c, dev_c, recv_c),
            base_d,
        ))

    flying = {}

    def window(start, rows):
        return pl.ds(pl.multiple_of(start, TILE_ROWS), rows)

    def push(p, level):
        rows, _, other, device, landing = plans[p][level]
        part = window(other, rows)
        send[p, :, part, :] = total[p, :, part, :].astype(BF16)
        flying[p, level] = remote(
            send.at[p, :, part, :], landing.at[p], rs_s.at[p, level], rs_r.at[p, level], device
        )

    def take(p, level):
        rows, base, _, _, landing = plans[p][level]
        flying[p, level].wait()
        part = window(base, rows)
        total[p, :, part, :] += landing[p].astype(F32)

    def push_z(p):
        base_c = plans[p][2][1]
        part = window(base_c, rows_c)
        send[p, :, part, :] = total[p, :, part, :].astype(BF16)
        for step in range(1, nz):
            there = base_c + lax.rem(z + step, nz) * rows_d
            flying[p, 2 + step] = remote(
                send.at[p, :, window(there, rows_d), :], recv_d.at[p, step - 1],
                rs_s.at[p, 2 + step], rs_r.at[p, 2 + step], to_z(step),
            )

    def take_z(p):
        part = window(plans[p][3], rows_d)
        value = total[p, :, part, :]
        for step in range(1, nz):
            flying[p, 2 + step].wait()
            value = value + recv_d[p, step - 1].astype(F32)
        grads[p, :, part, :] = value.astype(BF16)
        for step in range(1, nz):
            flying[p, "z", step] = remote(
                grads.at[p, :, part, :], grads.at[p, :, part, :],
                ag_s.at[p, 2 + step], ag_r.at[p, 2 + step], to_z(step),
            )

    def spread(p, level):
        rows, base, _, device, _ = plans[p][level]
        part = window(base, rows)
        flying[p, "g", level] = remote(
            grads.at[p, :, part, :], grads.at[p, :, part, :],
            ag_s.at[p, level], ag_r.at[p, level], device,
        )

    def event(p, number):
        if number == 0:
            push(p, 0)
        elif number in (1, 2):
            take(p, number - 1)
            push(p, number)
        elif number == 3:
            take(p, 2)
            push_z(p)
        elif number == 4:
            take_z(p)
        elif number == 5:
            for step in range(1, nz):
                flying[p, "z", step].wait()
            spread(p, 2)
        elif number in (6, 7):
            flying[p, "g", 8 - number].wait()
            spread(p, 7 - number)
        elif number == 8:
            flying[p, "g", 0].wait()

    starts = (12, 17, 21, 25, 29, 35, 38)
    due = sorted(
        (slot, p, number)
        for p in range(pairs)
        for number, slot in enumerate((4 + 4 * p, 7 + 4 * p) + tuple(s + 5 * p for s in starts))
    )

    def tick(slot):
        while reduced and due and due[0][0] <= slot:
            _, p, number = due.pop(0)
            event(p, number)

    def input_block(i):
        here = pl.ds(i * win, win)
        there = pl.ds((i + 1) * win, win)
        value = nt(dq[here], w_q[...]) + nt(dk[there], w_k[...]) + nt(dv[there], w_v[...])
        if i in (0, blocks - 1):
            for side in (1,) if i == 0 else (0,):
                part_k = jnp.concatenate([side_recv[p, side, 0] for p in range(pairs)], axis=1)
                part_v = jnp.concatenate([side_recv[p, side, 1] for p in range(pairs)], axis=1)
                value = value + nt(part_k, w_k[...]) + nt(part_v, w_v[...])
        out[here] = value.astype(BF16)

    slot = 0
    for p in range(pairs):
        for i in (0, blocks - 1):
            tick(slot)
            attend(p, i)
            slot += 2
        finish(p)
    for i in range(1, blocks - 1):
        tick(slot)
        input_block(i)
        slot += 1
    tick(blocks * pairs + 10)
    for copy in sides:
        copy.wait()
    input_block(0)
    input_block(blocks - 1)
    tick(1000)


def lay_out(total, grads, out, g_q, g_k, g_v, g_o, sem):
    pairs, _, width, _ = grads.shape
    copies = [(total, out)]
    for p in range(pairs):
        cols = pl.ds(p * PAIR, PAIR)
        copies += [(grads.at[p, m], g.at[:, cols]) for m, g in enumerate((g_q, g_k, g_v))]
        for j in range(width // PAIR):
            block = pl.ds(j * PAIR, PAIR)
            copies.append((grads.at[p, 3, block], g_o.at[cols, block]))
    flying = [pltpu.make_async_copy(src, dst, sem.at[n]) for n, (src, dst) in enumerate(copies)]
    for copy in flying:
        copy.start()
    for copy in flying:
        copy.wait()


def on_device(tokens, segment_ids, w_query, w_key, w_value, w_out, grad_out):
    span, width = tokens.shape[1:]
    n_ctx, n_dp = lax.axis_size("ctx"), lax.axis_size("dp")
    pairs = width // PAIR
    nz = n_ctx // 2
    reduced = n_dp == 4 and n_ctx % 2 == 0 and width // (8 * nz) >= TILE_ROWS
    ext = span + 2 * WINDOW
    vmem = pltpu.VMEM
    dma = pltpu.SemaphoreType.DMA
    few = nz if reduced else 2

    def red(*shape):
        return vmem(shape if reduced else (TILE_ROWS, 128), BF16)

    weights = vmem((width, width), BF16)
    scratch = [
        vmem((span, width), BF16),
        vmem((1, span), jnp.int32),
        weights, weights, weights, weights,
        vmem((span, width), BF16),
        dma((7,)),
        vmem((2, WINDOW, width), BF16),
        vmem((2, 8, span), jnp.int32),
        vmem((8, span), jnp.int32),
        vmem((width, ext), BF16),
        vmem((span, width), BF16),
        vmem((span, width), BF16),
        vmem((ext, width), BF16),
        vmem((ext, width), BF16),
        vmem((span // WINDOW, WINDOW, 3 * WINDOW), F32),
        vmem((span, width), BF16),
        vmem((ext, width), BF16),
        vmem((ext, width), BF16),
        vmem((pairs, ext, PAIR), F32),
        vmem((pairs, ext, PAIR), F32),
        vmem((pairs, span, PAIR), BF16),
        vmem((pairs, 2, 2, WINDOW, PAIR), BF16),
        vmem((pairs, 2, 2, WINDOW, PAIR), BF16),
        vmem((pairs, 4, width, PAIR) if reduced else (8, 128), F32),
        red(pairs, 4, width, PAIR),
        red(pairs, 4, width // 2, PAIR),
        red(pairs, 4, width // 4, PAIR),
        red(pairs, 4, width // 8, PAIR),
        red(pairs, few - 1, 4, width // (8 * few), PAIR),
        dma((2,)), dma((2,)), dma((2,)), dma((2,)),
        dma((pairs, 2)), dma((pairs, 2)),
        dma((pairs, 2 + few)), dma((pairs, 2 + few)),
        dma((pairs, 2 + few)), dma((pairs, 2 + few)),
    ]
    total, grads = pl.pallas_call(
        functools.partial(kernel, n_ctx, n_dp, reduced),
        out_shape=(
            jax.ShapeDtypeStruct((span, width), BF16),
            jax.ShapeDtypeStruct((pairs, 4, width, PAIR), BF16 if reduced else F32),
        ),
        in_specs=[pl.BlockSpec(memory_space=pl.ANY)] * 7,
        out_specs=(pl.BlockSpec(memory_space=pltpu.VMEM),) * 2,
        scratch_shapes=scratch,
        compiler_params=pltpu.CompilerParams(
            collective_id=0, has_side_effects=True, vmem_limit_bytes=60 * 1024 * 1024
        ),
    )(tokens[0], segment_ids, w_query, w_key, w_value, w_out, grad_out[0])
    if not reduced:
        grads = lax.psum(grads, ("ctx", "dp")).astype(BF16)
    square = jax.ShapeDtypeStruct((width, width), BF16)
    total, *grads = pl.pallas_call(
        lay_out,
        out_shape=(jax.ShapeDtypeStruct((span, width), BF16),) + (square,) * 4,
        in_specs=[pl.BlockSpec(memory_space=pltpu.VMEM)] * 2,
        out_specs=(pl.BlockSpec(memory_space=pl.ANY),) * 5,
        scratch_shapes=[dma((1 + pairs * (3 + width // PAIR),))],
    )(total, grads)
    return (total[None], *grads)


def solution(mesh):
    return jax.shard_map(
        on_device,
        mesh=mesh,
        in_specs=(P("dp", "ctx", None), P("dp", "ctx"), P(), P(), P(), P(), P("dp", "ctx", None)),
        out_specs=(P("dp", "ctx", None), P(), P(), P(), P()),
        check_vma=False,
    )
```

```python
import functools

import jax
import jax.numpy as jnp
from jax import lax
from jax.experimental import pallas as pl
from jax.experimental.pallas import tpu as pltpu
from jax.sharding import PartitionSpec as P

HD = 64
WINDOW = 128
PAIR = 128
TILE_ROWS = 16
MESH = pl.DeviceIdType.MESH
F32 = jnp.float32
BF16 = jnp.bfloat16


def nn(left, right):
    return lax.dot_general(left, right, (((1,), (0,)), ((), ())), preferred_element_type=F32)


def nt(left, right):
    return lax.dot_general(left, right, (((1,), (1,)), ((), ())), preferred_element_type=F32)


def tn(left, right):
    return lax.dot_general(left, right, (((0,), (0,)), ((), ())), preferred_element_type=F32)


def wrap(index, count):
    return lax.rem(index + count, count)


def kernel(
    n_ctx, n_dp, reduced,
    tok_hbm, seg_hbm, wq_hbm, wk_hbm, wv_hbm, wo_hbm, dout_hbm,
    out, grads,
    tok, seg_row, w_q, w_k, w_v, w_o, dout, load,
    halo, seg_halo, seg_own, tok_t, query, dattn, keyed, valued, bias,
    dq, dk, dv, acc_k, acc_v, att,
    side_send, side_recv,
    total, send, recv_a, recv_b, recv_c, recv_d,
    halo_s, halo_r, seg_s, seg_r, side_s, side_r, rs_s, rs_r, ag_s, ag_r,
):
    span, width = tok.shape
    win = WINDOW
    loads = {}
    for n, (name, src, dst) in enumerate((
        ("seg", seg_hbm, seg_row), ("tok", tok_hbm, tok), ("q", wq_hbm, w_q), ("k", wk_hbm, w_k),
        ("v", wv_hbm, w_v), ("o", wo_hbm, w_o), ("dout", dout_hbm, dout),
    )):
        loads[name] = pltpu.make_async_copy(src, dst, load.at[n])
        loads[name].start()
    blocks = span // win
    pairs = width // PAIR
    ctx = lax.axis_index("ctx")
    dp = lax.axis_index("dp")
    up = (wrap(ctx + 1, n_ctx), dp)
    down = (wrap(ctx - 1, n_ctx), dp)

    core = lax.rem(dp, 2)
    y = lax.div(dp, 2)
    x = lax.rem(ctx, 2)
    z = lax.div(ctx, 2)
    nz = n_ctx // 2
    to_core = (ctx, dp + 1 - 2 * core)
    to_y = (ctx, lax.rem(dp + 2, 4))
    to_x = (ctx + 1 - 2 * x, dp)

    def to_z(step):
        return (lax.rem(ctx + 2 * step, n_ctx), dp)

    partners = [up, down]
    if reduced:
        partners += [to_core, to_y] + [to_z(step) for step in range(1, nz)]
    barrier = pltpu.get_barrier_semaphore()
    for partner in partners:
        pl.semaphore_signal(barrier, inc=1, device_id=partner, device_id_type=MESH)

    loads["seg"].wait()
    seg_own[...] = jnp.broadcast_to(seg_row[...], seg_own.shape)
    pl.semaphore_wait(barrier, len(partners))

    def remote(src, dst, s, r, device):
        copy = pltpu.make_async_remote_copy(
            src_ref=src, dst_ref=dst, send_sem=s, recv_sem=r, device_id=device, device_id_type=MESH
        )
        copy.start()
        return copy

    first = [
        remote(tok_hbm.at[pl.ds(span - win, win)], halo.at[0], halo_s.at[0], halo_r.at[0], up),
        remote(tok_hbm.at[pl.ds(0, win)], halo.at[1], halo_s.at[1], halo_r.at[1], down),
        remote(seg_own, seg_halo.at[0], seg_s.at[0], seg_r.at[0], up),
        remote(seg_own, seg_halo.at[1], seg_s.at[1], seg_r.at[1], down),
    ]

    loads["tok"].wait()
    tok_t[:, pl.ds(win, span)] = tok[...].T
    loads["q"].wait()
    query[...] = nn(tok[...], w_q[...]).astype(BF16)
    loads["k"].wait()
    keyed[pl.ds(win, span)] = nn(tok[...], w_k[...]).astype(BF16)
    loads["v"].wait()
    valued[pl.ds(win, span)] = nn(tok[...], w_v[...]).astype(BF16)
    loads["o"].wait()
    loads["dout"].wait()
    dattn[...] = nt(dout[...], w_o[...]).astype(BF16)

    scale = float(HD) ** (-0.5)
    lane = lax.broadcasted_iota(jnp.int32, (win, PAIR), 1)
    left = lane < HD

    def stack(rows):
        zero = jnp.zeros_like(rows)
        return jnp.concatenate([jnp.where(left, rows, zero), jnp.where(left, zero, rows)], axis=0)

    def join(rows):
        return jnp.where(left, rows[:win], rows[win:])

    def attend(p, i):
        cols = pl.ds(p * PAIR, PAIR)
        here = pl.ds(i * win, win)
        around = pl.ds(i * win, 3 * win)
        q2 = stack(query[here, cols])
        d2 = stack(dattn[here, cols])
        k2 = keyed[around, cols]
        v2 = valued[around, cols]
        mask = bias[i]
        score = nt(q2, k2) * scale + jnp.concatenate([mask, mask], axis=0)
        top = jnp.max(score, axis=-1, keepdims=True)
        weight = jnp.exp(score - top)
        prob = weight * (1.0 / jnp.sum(weight, axis=-1, keepdims=True))
        probb = prob.astype(BF16)
        attended = nn(probb, v2).astype(BF16)
        att[p, here, :] = join(attended)
        delta = jnp.sum(d2.astype(F32) * attended.astype(F32), axis=-1, keepdims=True)
        dscore = (prob * (nt(d2, v2) - delta)).astype(BF16)
        dq[here, cols] = (join(nn(dscore, k2)) * scale).astype(BF16)
        part_k = tn(dscore, q2)
        part_v = tn(probb, d2)
        acc_k[p, around] += part_k
        acc_v[p, around] += part_v

    own = seg_row[...].astype(F32)
    q_pos = lax.broadcasted_iota(jnp.int32, (win, 3 * win), 0)
    k_pos = lax.broadcasted_iota(jnp.int32, (win, 3 * win), 1)
    near = (k_pos >= q_pos) & (k_pos <= q_pos + 2 * win)

    def masked(i, keys):
        column = jnp.broadcast_to(own[:, i * win : (i + 1) * win], (win, win)).T
        column = jnp.concatenate([column] * 3, axis=1)
        bias[i] = jnp.where(near & (column == keys), 0.0, -1e30)

    acc_k[...] = jnp.zeros_like(acc_k)
    acc_v[...] = jnp.zeros_like(acc_v)
    for i in range(1, blocks - 1):
        masked(i, own[:, (i - 1) * win : (i + 2) * win])
        for p in range(pairs):
            attend(p, i)

    for copy in first:
        copy.wait()
    for side, start in ((0, 0), (1, win + span)):
        rows = halo[side]
        keyed[pl.ds(start, win)] = nn(rows, w_k[...]).astype(BF16)
        valued[pl.ds(start, win)] = nn(rows, w_v[...]).astype(BF16)
        tok_t[:, pl.ds(start, win)] = rows.T
    low = jnp.where(ctx > 0, seg_halo[0, 0:1, span - win :].astype(F32), -1.0)
    high = jnp.where(ctx < n_ctx - 1, seg_halo[1, 0:1, :win].astype(F32), -1.0)
    masked(0, jnp.concatenate([low, own[:, : 2 * win]], axis=1))
    masked(blocks - 1, jnp.concatenate([own[:, span - 2 * win :], high], axis=1))

    sides = []

    def finish(p):
        cols = pl.ds(p * PAIR, PAIR)
        dk[:, cols] = (acc_k[p] * scale).astype(BF16)
        dv[:, cols] = acc_v[p].astype(BF16)
        for side, start, device in ((0, 0, down), (1, win + span, up)):
            side_send[p, side, 0] = dk[pl.ds(start, win), cols]
            side_send[p, side, 1] = dv[pl.ds(start, win), cols]
            sides.append(
                remote(
                    side_send.at[p, side], side_recv.at[p, side],
                    side_s.at[p, side], side_r.at[p, side], device,
                )
            )
        values = (
            nn(tok_t[:, pl.ds(win, span)], dq[:, cols]),
            nn(tok_t[...], dk[:, cols]),
            nn(tok_t[...], dv[:, cols]),
        )
        place = total if reduced else grads
        for m, value in enumerate(values):
            place[p, m] = value
        value = tn(att[p], dout[...])
        for j in range(width // PAIR):
            block = pl.ds(j * PAIR, PAIR)
            place[p, 3, block] = value[:, j * PAIR : (j + 1) * PAIR]

    rows_a, rows_b, rows_c = width // 2, width // 4, width // 8
    rows_d = width // (8 * nz)
    plans = []
    for p in range(pairs):
        (bit_b, dev_b), (bit_c, dev_c) = ((y, to_y), (x, to_x))
        base_a = core * rows_a
        base_b = base_a + bit_b * rows_b
        base_c = base_b + bit_c * rows_c
        base_d = base_c + z * rows_d
        plans.append((
            (rows_a, base_a, (1 - core) * rows_a, to_core, recv_a),
            (rows_b, base_b, base_a + (1 - bit_b) * rows_b, dev_b, recv_b),
            (rows_c, base_c, base_b + (1 - bit_c) * rows_c, dev_c, recv_c),
            base_d,
        ))

    flying = {}

    def window(start, rows):
        return pl.ds(pl.multiple_of(start, TILE_ROWS), rows)

    def push(p, level):
        rows, _, other, device, landing = plans[p][level]
        part = window(other, rows)
        send[p, :, part, :] = total[p, :, part, :].astype(BF16)
        flying[p, level] = remote(
            send.at[p, :, part, :], landing.at[p], rs_s.at[p, level], rs_r.at[p, level], device
        )

    def take(p, level):
        rows, base, _, _, landing = plans[p][level]
        flying[p, level].wait()
        part = window(base, rows)
        total[p, :, part, :] += landing[p].astype(F32)

    def push_z(p):
        base_c = plans[p][2][1]
        part = window(base_c, rows_c)
        send[p, :, part, :] = total[p, :, part, :].astype(BF16)
        for step in range(1, nz):
            there = base_c + lax.rem(z + step, nz) * rows_d
            flying[p, 2 + step] = remote(
                send.at[p, :, window(there, rows_d), :], recv_d.at[p, step - 1],
                rs_s.at[p, 2 + step], rs_r.at[p, 2 + step], to_z(step),
            )

    def take_z(p):
        part = window(plans[p][3], rows_d)
        value = total[p, :, part, :]
        for step in range(1, nz):
            flying[p, 2 + step].wait()
            value = value + recv_d[p, step - 1].astype(F32)
        grads[p, :, part, :] = value.astype(BF16)
        for step in range(1, nz):
            flying[p, "z", step] = remote(
                grads.at[p, :, part, :], grads.at[p, :, part, :],
                ag_s.at[p, 2 + step], ag_r.at[p, 2 + step], to_z(step),
            )

    def spread(p, level):
        rows, base, _, device, _ = plans[p][level]
        part = window(base, rows)
        flying[p, "g", level] = remote(
            grads.at[p, :, part, :], grads.at[p, :, part, :],
            ag_s.at[p, level], ag_r.at[p, level], device,
        )

    def event(p, number):
        if number == 0:
            push(p, 0)
        elif number in (1, 2):
            take(p, number - 1)
            push(p, number)
        elif number == 3:
            take(p, 2)
            push_z(p)
        elif number == 4:
            take_z(p)
        elif number == 5:
            for step in range(1, nz):
                flying[p, "z", step].wait()
            spread(p, 2)
        elif number in (6, 7):
            flying[p, "g", 8 - number].wait()
            spread(p, 7 - number)
        elif number == 8:
            flying[p, "g", 0].wait()

    starts = (12, 17, 21, 25, 29, 35, 38)
    due = sorted(
        (slot, p, number)
        for p in range(pairs)
        for number, slot in enumerate((4 + 4 * p, 7 + 4 * p) + tuple(s + 5 * p for s in starts))
    )

    def tick(slot):
        while reduced and due and due[0][0] <= slot:
            _, p, number = due.pop(0)
            event(p, number)

    def input_block(i):
        here = pl.ds(i * win, win)
        there = pl.ds((i + 1) * win, win)
        value = nt(dq[here], w_q[...]) + nt(dk[there], w_k[...]) + nt(dv[there], w_v[...])
        if i in (0, blocks - 1):
            for side in (1,) if i == 0 else (0,):
                part_k = jnp.concatenate([side_recv[p, side, 0] for p in range(pairs)], axis=1)
                part_v = jnp.concatenate([side_recv[p, side, 1] for p in range(pairs)], axis=1)
                value = value + nt(part_k, w_k[...]) + nt(part_v, w_v[...])
        out[here] = value.astype(BF16)

    slot = 0
    for p in range(pairs):
        for i in (0, blocks - 1):
            tick(slot)
            attend(p, i)
            slot += 2
        finish(p)
    for i in range(1, blocks - 1):
        tick(slot)
        input_block(i)
        slot += 1
    tick(blocks * pairs + 10)
    for copy in sides:
        copy.wait()
    input_block(0)
    input_block(blocks - 1)
    tick(1000)


def lay_out(total, grads, out, g_q, g_k, g_v, g_o, sem):
    pairs, _, width, _ = grads.shape
    copies = [(total, out)]
    for p in range(pairs):
        cols = pl.ds(p * PAIR, PAIR)
        copies += [(grads.at[p, m], g.at[:, cols]) for m, g in enumerate((g_q, g_k, g_v))]
        for j in range(width // PAIR):
            block = pl.ds(j * PAIR, PAIR)
            copies.append((grads.at[p, 3, block], g_o.at[cols, block]))
    flying = [pltpu.make_async_copy(src, dst, sem.at[n]) for n, (src, dst) in enumerate(copies)]
    for copy in flying:
        copy.start()
    for copy in flying:
        copy.wait()


def on_device(tokens, segment_ids, w_query, w_key, w_value, w_out, grad_out):
    span, width = tokens.shape[1:]
    n_ctx, n_dp = lax.axis_size("ctx"), lax.axis_size("dp")
    pairs = width // PAIR
    nz = n_ctx // 2
    reduced = n_dp == 4 and n_ctx % 2 == 0 and width // (8 * nz) >= TILE_ROWS
    ext = span + 2 * WINDOW
    vmem = pltpu.VMEM
    dma = pltpu.SemaphoreType.DMA
    few = nz if reduced else 2

    def red(*shape):
        return vmem(shape if reduced else (TILE_ROWS, 128), BF16)

    weights = vmem((width, width), BF16)
    scratch = [
        vmem((span, width), BF16),
        vmem((1, span), jnp.int32),
        weights, weights, weights, weights,
        vmem((span, width), BF16),
        dma((7,)),
        vmem((2, WINDOW, width), BF16),
        vmem((2, 8, span), jnp.int32),
        vmem((8, span), jnp.int32),
        vmem((width, ext), BF16),
        vmem((span, width), BF16),
        vmem((span, width), BF16),
        vmem((ext, width), BF16),
        vmem((ext, width), BF16),
        vmem((span // WINDOW, WINDOW, 3 * WINDOW), F32),
        vmem((span, width), BF16),
        vmem((ext, width), BF16),
        vmem((ext, width), BF16),
        vmem((pairs, ext, PAIR), F32),
        vmem((pairs, ext, PAIR), F32),
        vmem((pairs, span, PAIR), BF16),
        vmem((pairs, 2, 2, WINDOW, PAIR), BF16),
        vmem((pairs, 2, 2, WINDOW, PAIR), BF16),
        vmem((pairs, 4, width, PAIR) if reduced else (8, 128), F32),
        red(pairs, 4, width, PAIR),
        red(pairs, 4, width // 2, PAIR),
        red(pairs, 4, width // 4, PAIR),
        red(pairs, 4, width // 8, PAIR),
        red(pairs, few - 1, 4, width // (8 * few), PAIR),
        dma((2,)), dma((2,)), dma((2,)), dma((2,)),
        dma((pairs, 2)), dma((pairs, 2)),
        dma((pairs, 2 + few)), dma((pairs, 2 + few)),
        dma((pairs, 2 + few)), dma((pairs, 2 + few)),
    ]
    total, grads = pl.pallas_call(
        functools.partial(kernel, n_ctx, n_dp, reduced),
        out_shape=(
            jax.ShapeDtypeStruct((span, width), BF16),
            jax.ShapeDtypeStruct((pairs, 4, width, PAIR), BF16 if reduced else F32),
        ),
        in_specs=[pl.BlockSpec(memory_space=pl.ANY)] * 7,
        out_specs=(pl.BlockSpec(memory_space=pltpu.VMEM),) * 2,
        scratch_shapes=scratch,
        compiler_params=pltpu.CompilerParams(
            collective_id=0, has_side_effects=True, vmem_limit_bytes=60 * 1024 * 1024
        ),
    )(tokens[0], segment_ids, w_query, w_key, w_value, w_out, grad_out[0])
    if not reduced:
        grads = lax.psum(grads, ("ctx", "dp")).astype(BF16)
    square = jax.ShapeDtypeStruct((width, width), BF16)
    total, *grads = pl.pallas_call(
        lay_out,
        out_shape=(jax.ShapeDtypeStruct((span, width), BF16),) + (square,) * 4,
        in_specs=[pl.BlockSpec(memory_space=pl.ANY)] * 2,
        out_specs=(pl.BlockSpec(memory_space=pl.ANY),) * 5,
        compiler_params=pltpu.CompilerParams(vmem_limit_bytes=60 * 1024 * 1024),
        scratch_shapes=[dma((1 + pairs * (3 + width // PAIR),))],
    )(total, grads)
    return (total[None], *grads)


def solution(mesh):
    return jax.shard_map(
        on_device,
        mesh=mesh,
        in_specs=(P("dp", "ctx", None), P("dp", "ctx"), P(), P(), P(), P(), P("dp", "ctx", None)),
        out_specs=(P("dp", "ctx", None), P(), P(), P(), P()),
        check_vma=False,
    )
```
